512 devices in a mesh: gx: 16 (over y, core), yz: 32 (over x, z).
Axes of the slice: x: 4, y: 8, z: 8, core: 2. Of those that a mesh axis runs over, the one named last changes fastest.
Arguments:
- stiffness: bfloat16 [16, 32, 8, 27, 9216], P('gx', 'yz'), may hold values from -0.625 to 0.625
- prolong: bfloat16 [16, 32, 8, 96, 128], P('gx', 'yz'), may hold values from -1.5 to 1.5
- kcol: int32 [16, 32, 8, 27], P('gx', 'yz'), may hold values from 0 to 15
- kcount: int32 [16, 32, 8], P('gx', 'yz'), may hold values from 24 to 27
- qslot: int32 [16, 32, 8, 27, 2], P('gx', 'yz'), may hold values from 0 to 2
- glist: int32 [16, 32, 4, 2], P('gx', 'yz'), may hold values from 0 to 7
- owner: int32 [16, 32, 16, 1], P('gx', 'yz'), may hold values from 0 to 31; in each aligned block of 16 rows (0 to 15, 16 to 31, ..., all dimensions but the last counted through in order) at most 2 rows name the same one
- dest: int32 [16, 32, 16, 3], P('gx', 'yz'), may hold values from 0 to 47
Outputs:
- coarse: float32 [16, 32, 48, 4096], P('gx', 'yz')
The draws below stay inside these ranges and needn't reach their ends.
Inputs may be any that keep to these rules, and one draw needn't show every extreme that they name: Among the 16 pairs of one device no owner occurs more than 2 times; some device has an owner exactly 2 times, and every owner occurs somewhere.
All inputs are finite; a program needn't handle non-finite values.
Results may differ from the reference program's by a relative error of at most 0.0029.
Values may be sent and summed in bfloat16 or wider, within the bound.
No kernel may reach another device: no remote copies, remote signals or barrier semaphores. Data moves between devices by JAX's collectives and lax.ppermute only.
A program may use at most 128 MiB of HBM per device.

```python
import math
import jax
import jax.numpy as jnp
import numpy as np
from jax import lax

BK = 96
BP = 64
KW = 27
PW = 2
QW = 3
NB = 8
G = 2
EXT = 16
M = 16
CAP = 2
NS = 48
N_GX = 16
N_YZ = 32


def set_ends(values, key, least, top_value):
    longest = values.shape.index(max(values.shape))
    spots = []
    for shift in (0, 1):
        where = [jax.random.randint(jax.random.fold_in(key, axis), (), 0, length) for axis, length in enumerate(values.shape)]
        where[longest] = (where[longest] + shift) % values.shape[longest]
        spots.append(tuple(where))
    return values.at[spots[0]].set(least).at[spots[1]].set(top_value)


def shard_levels(own_key, extent, split, smallest, top_value):
    def one(axis_at, shards_of):
        draws = jax.random.uniform(jax.random.fold_in(jax.random.fold_in(own_key, 6), axis_at), (shards_of,), jnp.float32, smallest / len(split), top_value / len(split))
        return jnp.repeat(jnp.exp(draws), extent[axis_at] // shards_of).reshape((-1,) + (1,) * (len(extent) - axis_at - 1))

    gain = one(*split[0])
    for cut in split[1:]:
        gain = gain * one(*cut)
    return gain


def shared_out(stream_key, own, number, rows, amount, top, bound, skew):
    ranking = jax.random.permutation(stream_key, amount)
    packed, ordinary = shares(amount, rows * top, bound, skew, True), shares(amount, rows * top, bound, skew, False)
    places = jnp.arange(amount)

    def named(tallies, turn):
        used = int((tallies > 0).sum())
        fixed = max(1, used // 4)
        moved = fixed + (places - fixed + turn * (used - fixed)) % max(1, amount - fixed)
        return jnp.zeros((amount,), jnp.int32).at[ranking[jnp.where(places < fixed, places, moved)]].set(jnp.asarray(tallies, jnp.int32))

    tallies = jnp.where(number % 4 == 0, named(packed, number // 4), named(ordinary, number - number // 4 - 1))
    mixed = jax.random.permutation(jax.random.fold_in(own, 3), amount)
    donor, receiver = mixed[0:amount // 2 * 2:2], mixed[1:amount // 2 * 2:2]
    room = jnp.minimum(tallies[donor] - 1, bound - tallies[receiver]) // 2
    room = jnp.where((donor == ranking[0]) | (receiver == ranking[0]) | (tallies[receiver] == 0), 0, jnp.maximum(room, 0))
    moved = jax.random.randint(jax.random.fold_in(own, 4), (amount // 2,), 0, 1 << 20) % (room + 1)
    tallies = tallies.at[donor].add(-moved).at[receiver].add(moved)
    items = jnp.searchsorted(jnp.cumsum(tallies), jnp.arange(rows * top), side="right").astype(jnp.int32)
    listing = items.reshape(top, rows).T
    listing = listing[jax.random.permutation(jax.random.fold_in(own, 1), rows)]
    turn = jax.random.randint(jax.random.fold_in(own, 2), (rows, 1), 0, top)
    return jnp.take_along_axis(listing, (jnp.arange(top)[None, :] + turn) % top, axis=1)


def shares(number_of, total, most, lean, full):
    portions = [(1 << 20) // math.isqrt(rank ** lean) + 1 for rank in range(1, number_of + 1)]
    largest = most if full else min(most, max(-(-total // number_of), total * portions[0] // sum(portions)))
    least = 1 if total - largest >= number_of - 1 else 0
    holding, spare = [largest] + [least] * (number_of - 1), total - largest - least * (number_of - 1)
    while spare > 0:
        free = [i for i in range(1, number_of) if holding[i] < largest] or [i for i in range(1, number_of) if holding[i] < most]
        pool, remaining = sum([portions[i] for i in free]), spare
        for i in free:
            extra = min(most - holding[i], max(1, remaining * portions[i] // pool), spare)
            holding[i] = holding[i] + extra
            spare = spare - extra
    return np.array(holding)


def centred(key, shape, deviation, most, shards=(), dtype=jnp.bfloat16):
    array = jax.random.normal(key, shape, jnp.float32) * deviation
    if len(shards) > 0:
        array = shard_levels(key, shape, shards, -0.22, 0.18) * array
    return jnp.clip(array, min=-most, max=most).astype(dtype)


def setup_inputs(seed: int = 0) -> dict:
    key_of = jax.random.split(jax.random.key(seed), 9)
    stiffness = centred(key_of[0], (N_GX, N_YZ, NB, KW, BK * BK), BK ** -0.5, 0.625, ((0, 16), (1, 32)))
    prolong = centred(key_of[1], (N_GX, N_YZ, NB, BK, PW * BP), 0.25, 1.5, ((0, 16), (1, 32)))
    kcol = set_ends(jax.random.randint(key_of[2], (N_GX, N_YZ, NB, KW), 0, EXT), jax.random.fold_in(key_of[2], 1), 0, EXT - 1).astype(jnp.int32)
    kcount = set_ends(jax.random.randint(key_of[3], (N_GX, N_YZ, NB), KW - 3, KW + 1), jax.random.fold_in(key_of[3], 1), KW - 3, KW).astype(jnp.int32)
    qslot = set_ends(jax.random.randint(key_of[4], (N_GX, N_YZ, NB, KW, PW), 0, QW), jax.random.fold_in(key_of[4], 1), 0, QW - 1).astype(jnp.int32)
    glist = set_ends(jax.random.randint(key_of[5], (N_GX, N_YZ, 4, G), 0, NB), jax.random.fold_in(key_of[5], 1), 0, NB - 1).astype(jnp.int32)
    owner_keys = jax.random.split(jax.random.fold_in(key_of[6], 1), N_GX * N_YZ * M // M)
    owner_turns = jax.random.permutation(jax.random.fold_in(key_of[6], 3), N_GX * N_YZ * M // M)
    owner = jax.vmap(lambda own, number: shared_out(jax.random.fold_in(key_of[6], 2), own, number, M, N_YZ, 1, CAP, 2))(owner_keys, owner_turns).reshape((N_GX, N_YZ, M, 1))
    dest = set_ends(jax.random.randint(key_of[7], (N_GX, N_YZ, M, QW), 0, NS), jax.random.fold_in(key_of[7], 1), 0, NS - 1).astype(jnp.int32)
    return dict(stiffness=stiffness, prolong=prolong, kcol=kcol, kcount=kcount, qslot=qslot, glist=glist, owner=owner, dest=dest)


def pick_rows(prolong_dev, list_dev):
    return prolong_dev[list_dev]


def ghost_rows(prolong, glist):
    picked = jax.vmap(jax.vmap(pick_rows))(prolong, glist)
    zero_slab = jnp.zeros_like(picked[:1, :, 0])
    from_lower = jnp.concatenate([zero_slab, picked[:-1, :, 1]], 0)
    from_upper = jnp.concatenate([picked[1:, :, 0], zero_slab], 0)
    zero_column = jnp.zeros_like(picked[:, :1, 2])
    from_left = jnp.concatenate([zero_column, picked[:, :-1, 3]], 1)
    from_right = jnp.concatenate([picked[:, 1:, 2], zero_column], 1)
    return jnp.concatenate([prolong, from_lower, from_upper, from_left, from_right], 2)


def device_terms(operands):
    stiff_dev, extended_dev, kcol_dev, kcount_dev, qslot_dev, prolong_dev = operands
    row_count = stiff_dev.shape[0]
    square = stiff_dev.reshape(row_count, KW, BK, BK).astype(jnp.float32)
    gathered = extended_dev[kcol_dev].astype(jnp.float32)
    product = jnp.einsum('itab,itbc->itac', square, gathered)
    live_slot = (jnp.arange(KW)[None, :] < kcount_dev[:, None]).astype(jnp.float32)
    choose = (qslot_dev[..., None] == jnp.arange(QW)[None, None, None, :]).astype(jnp.float32)
    choose = choose * live_slot[:, :, None, None]
    split_terms = product.reshape(row_count, KW, BK, PW, BP)
    merged = jnp.einsum('itksc,itsq->ikqc', split_terms, choose).astype(jnp.bfloat16)
    merged = lax.optimization_barrier(merged).astype(jnp.float32)
    pair_blocks = prolong_dev.reshape(row_count, BK, PW, BP).astype(jnp.float32)
    terms = jnp.einsum('ikap,ikqc->iaqpc', pair_blocks, merged)
    return terms.reshape(row_count * PW, QW, BP * BP)


def slab_result(operands):
    stiff_slab, extended_slab, kcol_slab, kcount_slab, qslot_slab, prolong_slab, owner_slab, dest_slab = operands
    terms = lax.map(device_terms, (stiff_slab, extended_slab, kcol_slab, kcount_slab, qslot_slab, prolong_slab))
    index = (owner_slab[:, :, 0][:, :, None] * NS + dest_slab).astype(jnp.int32).reshape(-1)
    summed = jax.ops.segment_sum(terms.reshape(-1, BP * BP), index, num_segments=N_YZ * NS)
    return summed.reshape(N_YZ, NS, BP * BP)


def reference(stiffness, prolong, kcol, kcount, qslot, glist, owner, dest):
    extended = ghost_rows(prolong, glist)
    return lax.map(slab_result, (stiffness, extended, kcol, kcount, qslot, prolong, owner, dest))
```

```python
import functools
import jax
import jax.numpy as jnp
from jax import lax
from jax.experimental import pallas as pl
from jax.experimental.pallas import tpu as pltpu
from jax.sharding import PartitionSpec as P

BK = 96
BP = 64
KW = 27
PW = 2
QW = 3
NB = 8
G = 2
EXT = NB + 4 * G
M = NB * PW
NS = 48
CAP = 2
LANES = 128
PAIR_ROWS = QW * BP * BP // LANES
SEND_ROWS = CAP * PAIR_ROWS + 8
VMEM_LIMIT = 20 * 1024 * 1024


def pick_kernel(glist_ref, prolong_ref, *out_refs):
    for side, out_ref in enumerate(out_refs):
        for n in range(G):
            out_ref[n] = prolong_ref[glist_ref[n, side]]


def pick_rows(glist, prolong):
    piece = jax.ShapeDtypeStruct((G, BK, PW * BP), jnp.bfloat16)
    return pl.pallas_call(
        pick_kernel,
        out_shape=[piece] * 4,
        in_specs=[pl.BlockSpec(memory_space=pltpu.SMEM), pl.BlockSpec(memory_space=pltpu.VMEM)],
        out_specs=[pl.BlockSpec(memory_space=pltpu.VMEM)] * 4,
        compiler_params=pltpu.CompilerParams(vmem_limit_bytes=VMEM_LIMIT),
        name="pick_rows",
    )(glist, prolong)


def square_kernel(flat_ref, prolong_ref, out_ref, turned_ref, spread_ref):
    lane = lax.broadcasted_iota(jnp.int32, (BK // 4, LANES), 1)
    for t in range(KW):
        for c in range(BK * BK // LANES):
            spread_ref[t % 2, c * NB : (c + 1) * NB, :] = flat_ref[
                t, :, c * LANES : (c + 1) * LANES
            ].astype(jnp.float32)
        for i in range(NB):
            v0, v1, v2 = (
                spread_ref[t % 2, pl.ds(u * NB + i, BK // 4, stride=3 * NB), :] for u in range(3)
            )
            rows = [
                v0,
                pltpu.roll(jnp.where(lane >= 96, v0, v1), 32, 1),
                pltpu.roll(jnp.where(lane >= 64, v1, v2), 64, 1),
                pltpu.roll(v2, 96, 1),
            ]
            out_ref[i, :, t * LANES : (t + 1) * LANES] = jnp.concatenate(rows, 0).astype(
                jnp.bfloat16
            )
    r_from = lax.broadcasted_iota(jnp.int32, (BK, BK), 0)
    r_to = lax.broadcasted_iota(jnp.int32, (BK, BK), 1)
    row_order = (r_from == (r_to % (BK // 4)) * 4 + r_to // (BK // 4)).astype(jnp.bfloat16)
    c_to = lax.broadcasted_iota(jnp.int32, (LANES, LANES), 0)
    c_from = lax.broadcasted_iota(jnp.int32, (LANES, LANES), 1)
    in_pair = c_to % BP
    column_order = (
        c_from == c_to // BP * BP + (in_pair % (BP // 2)) * 2 + in_pair // (BP // 2)
    ).astype(jnp.bfloat16)
    for i in range(NB):
        turned = lax.dot_general(
            column_order, prolong_ref[i], (((1,), (1,)), ((), ())),
            preferred_element_type=jnp.float32,
        ).astype(jnp.bfloat16)
        turned_ref[i] = jnp.dot(
            turned, row_order, preferred_element_type=jnp.float32
        ).astype(jnp.bfloat16)


def square_blocks(flat, prolong):
    vmem = pl.BlockSpec(memory_space=pltpu.VMEM)
    return pl.pallas_call(
        square_kernel,
        out_shape=[
            jax.ShapeDtypeStruct((NB, BK, KW * LANES), jnp.bfloat16),
            jax.ShapeDtypeStruct((NB, LANES, BK), jnp.bfloat16),
        ],
        in_specs=[vmem] * 2,
        out_specs=[vmem] * 2,
        scratch_shapes=[pltpu.VMEM((2, BK * BK // LANES * NB, LANES), jnp.float32)],
        compiler_params=pltpu.CompilerParams(vmem_limit_bytes=VMEM_LIMIT),
        cost_estimate=pl.CostEstimate(flops=0, bytes_accessed=12_000_000, transcendentals=0),
        name="square_blocks",
    )(flat, prolong)


def terms_kernel(
    kcol_ref, kcount_ref, qslot_ref, owner_ref, dest_ref,
    square_ref, turned_ref, prolong_ref, g0_ref, g1_ref, g2_ref, g3_ref,
    send_ref,
    ext_ref, label_ref, count_ref,
):
    peers = send_ref.shape[0]
    lane = lax.broadcasted_iota(jnp.int32, (1, LANES), 1)
    left = lane < BP
    ext_ref[:NB] = prolong_ref[...]
    for n, ghost_ref in enumerate((g0_ref, g1_ref, g2_ref, g3_ref)):
        ext_ref[NB + n * G : NB + (n + 1) * G] = ghost_ref[...]
    label_ref[...] = jnp.full((peers, LANES), float(NS), jnp.float32)
    for o in range(peers):
        count_ref[o] = 0

    def one_row(i, carry):
        live = kcount_ref[i]
        merged = [jnp.zeros((BK, LANES), jnp.float32) for _ in range(QW)]
        for t in range(KW):
            q0 = jnp.where(t < live, qslot_ref[i, 0, t], QW)
            q1 = jnp.where(t < live, qslot_ref[i, 1, t], QW)
            product = jnp.dot(
                square_ref[i, :, t * LANES : t * LANES + BK],
                ext_ref[kcol_ref[i, t]],
                preferred_element_type=jnp.float32,
            )
            column = jnp.where(left, q0, q1)
            for q in range(QW):
                merged[q] += jnp.where(column == q, product, 0.0)
        merged = [part + pltpu.roll(part, BP, 1) for part in merged]
        merged = jnp.concatenate([jnp.where(left, merged[0], merged[1]), merged[2]], 1)
        terms = jnp.dot(
            turned_ref[i], merged.astype(jnp.bfloat16), preferred_element_type=jnp.float32
        )
        for a in range(PW):
            even = terms[a * BP : a * BP + BP // 2]
            odd = terms[a * BP + BP // 2 : (a + 1) * BP]
            even_01, even_2 = even[:, :LANES], even[:, LANES:]
            odd_01, odd_2 = odd[:, :LANES], odd[:, LANES:]
            tiles = [
                jnp.where(left, even_01, pltpu.roll(odd_01, BP, 1)),
                jnp.where(left, pltpu.roll(even_01, BP, 1), odd_01),
                jnp.where(left, even_2, odd_2),
            ]
            m = i * PW + a
            o = owner_ref[m]
            position = count_ref[o]
            count_ref[o] = position + 1
            base = pl.multiple_of(position * PAIR_ROWS, PAIR_ROWS)
            send_ref[o, pl.ds(base, PAIR_ROWS), :] = jnp.concatenate(tiles, 0).astype(jnp.bfloat16)
            label = label_ref[pl.ds(o, 1), :]
            for q in range(QW):
                label = jnp.where(
                    lane == position * QW + q, dest_ref[q, 0, m].astype(jnp.float32), label
                )
            label_ref[pl.ds(o, 1), :] = label
        return carry

    lax.fori_loop(0, NB, one_row, 0)
    for o in range(peers):
        send_ref[o, CAP * PAIR_ROWS :, :] = jnp.broadcast_to(
            label_ref[o : o + 1, :], (8, LANES)
        ).astype(jnp.bfloat16)


def make_terms(kcol, kcount, qslot, owner, dest, squares, turned, prolong, ghosts, peers):
    smem = pl.BlockSpec(memory_space=pltpu.SMEM)
    vmem = pl.BlockSpec(memory_space=pltpu.VMEM)
    return pl.pallas_call(
        terms_kernel,
        out_shape=jax.ShapeDtypeStruct((peers, SEND_ROWS, LANES), jnp.bfloat16),
        in_specs=[smem] * 5 + [vmem] * 7,
        out_specs=vmem,
        scratch_shapes=[
            pltpu.VMEM((EXT, BK, LANES), jnp.bfloat16),
            pltpu.VMEM((peers, LANES), jnp.float32),
            pltpu.SMEM((peers,), jnp.int32),
        ],
        compiler_params=pltpu.CompilerParams(vmem_limit_bytes=VMEM_LIMIT),
        cost_estimate=pl.CostEstimate(
            flops=1_000_000_000, bytes_accessed=8_000_000, transcendentals=0
        ),
        name="make_terms",
    )(kcol, kcount, qslot, owner, dest, squares, turned, prolong, *ghosts)


def sum_kernel(recv_ref, out_ref, acc_ref, label_ref, scalar_ref, sem):
    peers = recv_ref.shape[0]
    for s in range(peers):
        label_ref[s : s + 1, :] = recv_ref[s, CAP * PAIR_ROWS : CAP * PAIR_ROWS + 8, :].astype(
            jnp.float32
        )[:1].astype(jnp.int32)
    copy = pltpu.make_async_copy(label_ref, scalar_ref, sem)
    copy.start()
    rows = BP // 2
    acc_ref[...] = jnp.zeros_like(acc_ref)
    copy.wait()

    def add_source(s, carry):
        for slot in range(CAP):
            @pl.when(scalar_ref[s, slot * QW] < NS)
            def _():
                for q in range(QW):
                    n = scalar_ref[s, slot * QW + q]
                    start = pl.multiple_of(n * rows, rows)
                    base = slot * PAIR_ROWS + q * rows
                    acc_ref[pl.ds(start, rows), :] += recv_ref[s, base : base + rows, :].astype(
                        jnp.float32
                    )

        return carry

    lax.fori_loop(0, peers, add_source, 0)
    for n in range(0, NS, 8):
        for p in range(rows):
            out_ref[n : n + 8, p * LANES : (p + 1) * LANES] = acc_ref[
                pl.ds(n * rows + p, 8, stride=rows), :
            ]


def sum_terms(received):
    return pl.pallas_call(
        sum_kernel,
        out_shape=jax.ShapeDtypeStruct((NS, BP * BP), jnp.float32),
        in_specs=[pl.BlockSpec(memory_space=pltpu.VMEM)],
        out_specs=pl.BlockSpec(memory_space=pltpu.VMEM),
        scratch_shapes=[
            pltpu.VMEM((NS * BP // 2, LANES), jnp.float32),
            pltpu.VMEM((received.shape[0], LANES), jnp.int32),
            pltpu.SMEM((received.shape[0], LANES), jnp.int32),
            pltpu.SemaphoreType.DMA,
        ],
        compiler_params=pltpu.CompilerParams(vmem_limit_bytes=VMEM_LIMIT),
        name="sum_terms",
    )(received)


def on_device(stiffness, prolong, kcol, kcount, qslot, glist, owner, dest):
    prolong_rows = prolong[0, 0]
    picked = pick_rows(jnp.transpose(glist[0, 0]), prolong_rows)
    ghosts = []
    for axis, to_lower, to_upper in (("gx", 0, 1), ("yz", 2, 3)):
        size = lax.axis_size(axis)
        up = [(n, n + 1) for n in range(size - 1)]
        down = [(n + 1, n) for n in range(size - 1)]
        ghosts.append(lax.ppermute(picked[to_upper], axis, up))
        ghosts.append(lax.ppermute(picked[to_lower], axis, down))
    squares, turned = square_blocks(jnp.transpose(stiffness[0, 0], (1, 0, 2)), prolong_rows)
    packed = make_terms(
        kcol[0, 0],
        kcount[0, 0],
        jnp.transpose(qslot[0, 0], (0, 2, 1)),
        owner[0, 0, :, 0],
        jnp.transpose(dest[0, 0])[:, None, :],
        squares, turned, prolong_rows, ghosts, lax.axis_size("yz"),
    )
    received = lax.all_to_all(packed, "yz", split_axis=0, concat_axis=0, tiled=True)
    return sum_terms(received)[None, None]


def solution(mesh):
    split = ("gx", "yz")
    in_specs = tuple(P(*split, *(None,) * n) for n in (3, 3, 2, 1, 3, 2, 2, 2))
    return jax.shard_map(
        on_device, mesh=mesh, in_specs=in_specs, out_specs=P(*split, None, None), check_vma=False
    )
```

```python
import functools
import jax
import jax.numpy as jnp
from jax import lax
from jax.experimental import pallas as pl
from jax.experimental.pallas import tpu as pltpu
from jax.sharding import PartitionSpec as P

BK = 96
BP = 64
KW = 27
PW = 2
QW = 3
NB = 8
G = 2
EXT = NB + 4 * G
M = NB * PW
NS = 48
LANES = 128
TERMS = M * QW
PIECES = BP * BP // LANES
SEND_ROWS = TERMS + 8
FLAT_PARTS = ((0, 6), (6, 9), (15, 12))
SUM_OWNERS = 4
VMEM_LIMIT = 20 * 1024 * 1024


def pick_kernel(glist_hbm, prolong_hbm, *refs):
    out_refs, (glist_ref, prolong_ref, sem) = refs[:4], refs[4:]
    copies = [
        pltpu.make_async_copy(glist_hbm, glist_ref, sem.at[0]),
        pltpu.make_async_copy(prolong_hbm, prolong_ref, sem.at[1]),
    ]
    for copy in copies:
        copy.start()
    for copy in copies:
        copy.wait()
    for side, out_ref in enumerate(out_refs):
        for n in range(G):
            out_ref[n] = prolong_ref[glist_ref[n, side]]


def pick_rows(glist, prolong):
    piece = jax.ShapeDtypeStruct((G, BK, PW * BP), jnp.bfloat16)
    return pl.pallas_call(
        pick_kernel,
        out_shape=[piece] * 4,
        in_specs=[pl.BlockSpec(memory_space=pltpu.HBM)] * 2,
        out_specs=[pl.BlockSpec(memory_space=pltpu.VMEM)] * 4,
        scratch_shapes=[
            pltpu.SMEM((G, 4), jnp.int32),
            pltpu.VMEM((NB, BK, PW * BP), jnp.bfloat16),
            pltpu.SemaphoreType.DMA((2,)),
        ],
        compiler_params=pltpu.CompilerParams(vmem_limit_bytes=VMEM_LIMIT),
        name="pick_rows",
    )(*(pltpu.with_memory_space_constraint(x, pltpu.HBM) for x in (glist, prolong)))


def square_kernel(
    flat_hbm, prolong_hbm, out_ref, turned_ref, prolong_ref, flat_ref, spread_ref, flat_sem, sem
):
    flat_copies = [
        pltpu.make_async_copy(flat_hbm.at[t : t + n], flat_ref.at[t : t + n], flat_sem.at[part])
        for part, (t, n) in enumerate(FLAT_PARTS)
    ]
    prolong_copy = pltpu.make_async_copy(prolong_hbm, prolong_ref, sem)
    prolong_copy.start()
    for copy in flat_copies:
        copy.start()
    prolong_copy.wait()
    r_from = lax.broadcasted_iota(jnp.int32, (BK, BK), 0)
    r_to = lax.broadcasted_iota(jnp.int32, (BK, BK), 1)
    row_order = (r_from == (r_to % (BK // 4)) * 4 + r_to // (BK // 4)).astype(jnp.bfloat16)
    c_to = lax.broadcasted_iota(jnp.int32, (LANES, LANES), 0)
    c_from = lax.broadcasted_iota(jnp.int32, (LANES, LANES), 1)
    in_pair = c_to % BP
    column_order = (
        c_from == c_to // BP * BP + (in_pair % (BP // 2)) * 2 + in_pair // (BP // 2)
    ).astype(jnp.bfloat16)
    for i in range(NB):
        turned = lax.dot_general(
            column_order, prolong_ref[i], (((1,), (1,)), ((), ())),
            preferred_element_type=jnp.float32,
        ).astype(jnp.bfloat16)
        turned_ref[i] = jnp.dot(
            turned, row_order, preferred_element_type=jnp.float32
        ).astype(jnp.bfloat16)
    lane = lax.broadcasted_iota(jnp.int32, (BK // 4, LANES), 1)
    for t in range(KW):
        for part, (first, _) in enumerate(FLAT_PARTS):
            if t == first:
                flat_copies[part].wait()
        for c in range(BK * BK // LANES):
            spread_ref[t % 2, c * NB : (c + 1) * NB, :] = flat_ref[
                t, :, c * LANES : (c + 1) * LANES
            ].astype(jnp.float32)
        for i in range(NB):
            v0, v1, v2 = (
                spread_ref[t % 2, pl.ds(u * NB + i, BK // 4, stride=3 * NB), :] for u in range(3)
            )
            rows = [
                v0,
                pltpu.roll(jnp.where(lane >= 96, v0, v1), 32, 1),
                pltpu.roll(jnp.where(lane >= 64, v1, v2), 64, 1),
                pltpu.roll(v2, 96, 1),
            ]
            out_ref[i, :, t * LANES : (t + 1) * LANES] = jnp.concatenate(rows, 0).astype(
                jnp.bfloat16
            )


def square_blocks(flat, prolong):
    vmem = pl.BlockSpec(memory_space=pltpu.VMEM)
    return pl.pallas_call(
        square_kernel,
        out_shape=[
            jax.ShapeDtypeStruct((NB, BK, KW * LANES), jnp.bfloat16),
            jax.ShapeDtypeStruct((NB, LANES, BK), jnp.bfloat16),
            jax.ShapeDtypeStruct((NB, BK, LANES), jnp.bfloat16),
        ],
        in_specs=[pl.BlockSpec(memory_space=pltpu.HBM)] * 2,
        out_specs=[vmem] * 3,
        scratch_shapes=[
            pltpu.VMEM((KW, NB, BK * BK), jnp.bfloat16),
            pltpu.VMEM((2, BK * BK // LANES * NB, LANES), jnp.float32),
            pltpu.SemaphoreType.DMA((len(FLAT_PARTS),)),
            pltpu.SemaphoreType.DMA,
        ],
        compiler_params=pltpu.CompilerParams(vmem_limit_bytes=VMEM_LIMIT),
        cost_estimate=pl.CostEstimate(flops=0, bytes_accessed=12_000_000, transcendentals=0),
        name="square_blocks",
    )(*(pltpu.with_memory_space_constraint(x, pltpu.HBM) for x in (flat, prolong)))


def terms_kernel(
    kcol_hbm, kcount_hbm, qslot_hbm, owner_hbm, dest_hbm,
    square_ref, turned_ref, prolong_ref, g0_ref, g1_ref, g2_ref, g3_ref,
    send_ref,
    ext_ref, terms_ref, kcol_ref, kcount_ref, qslot_ref, owner_ref, dest_ref, sem,
):
    copies = [
        pltpu.make_async_copy(source, target, sem.at[n])
        for n, (source, target) in enumerate(
            (
                (kcol_hbm, kcol_ref),
                (kcount_hbm, kcount_ref),
                (qslot_hbm, qslot_ref),
                (owner_hbm, owner_ref),
                (dest_hbm, dest_ref),
            )
        )
    ]
    for copy in copies:
        copy.start()
    lane = lax.broadcasted_iota(jnp.int32, (1, LANES), 1)
    left = lane < BP
    ext_ref[:NB] = prolong_ref[...]
    for n, ghost_ref in enumerate((g0_ref, g1_ref, g2_ref, g3_ref)):
        ext_ref[NB + n * G : NB + (n + 1) * G] = ghost_ref[...]

    for copy in copies:
        copy.wait()

    def one_row(i, carry):
        live = kcount_ref[i]
        merged = [jnp.zeros((BK, LANES), jnp.float32) for _ in range(QW)]
        for t in range(KW):
            q0 = jnp.where(t < live, qslot_ref[i, 0, t], QW)
            q1 = jnp.where(t < live, qslot_ref[i, 1, t], QW)
            product = jnp.dot(
                square_ref[i, :, t * LANES : t * LANES + BK],
                ext_ref[kcol_ref[i, t]],
                preferred_element_type=jnp.float32,
            )
            column = jnp.where(left, q0, q1)
            for q in range(QW):
                merged[q] += jnp.where(column == q, product, 0.0)
        merged = [part + pltpu.roll(part, BP, 1) for part in merged]
        merged = jnp.concatenate([jnp.where(left, merged[0], merged[1]), merged[2]], 1)
        terms = jnp.dot(
            turned_ref[i], merged.astype(jnp.bfloat16), preferred_element_type=jnp.float32
        )
        for a in range(PW):
            even = terms[a * BP : a * BP + BP // 2]
            odd = terms[a * BP + BP // 2 : (a + 1) * BP]
            even_01, even_2 = even[:, :LANES], even[:, LANES:]
            odd_01, odd_2 = odd[:, :LANES], odd[:, LANES:]
            tiles = [
                jnp.where(left, even_01, pltpu.roll(odd_01, BP, 1)),
                jnp.where(left, pltpu.roll(even_01, BP, 1), odd_01),
                jnp.where(left, even_2, odd_2),
            ]
            start = pl.multiple_of((i * PW + a) * QW * PIECES, QW * PIECES)
            terms_ref[pl.ds(start, QW * PIECES), :] = jnp.concatenate(tiles, 0)
        return carry

    lax.fori_loop(0, NB, one_row, 0)
    row = lax.broadcasted_iota(jnp.int32, (8, LANES), 0)
    labels = jnp.zeros((8, LANES), jnp.float32)
    for m in range(M):
        owner = owner_ref[m].astype(jnp.float32)
        for q in range(QW):
            pair = jnp.where(row == 0, owner, dest_ref[0, q, 0, m].astype(jnp.float32))
            labels = jnp.where(lane == m * QW + q, pair, labels)
    labels = labels.astype(jnp.bfloat16)
    for piece in range(PIECES):
        send_ref[piece, :TERMS, :] = jnp.concatenate(
            [
                terms_ref[pl.ds(n * PIECES + piece, 8, stride=PIECES), :]
                for n in range(0, TERMS, 8)
            ],
            0,
        ).astype(jnp.bfloat16)
        send_ref[piece, TERMS:, :] = labels


def make_terms(kcol, kcount, qslot, owner, dest, squares, turned, prolong, ghosts):
    hbm = pl.BlockSpec(memory_space=pltpu.HBM)
    vmem = pl.BlockSpec(memory_space=pltpu.VMEM)
    numbers = [
        pltpu.with_memory_space_constraint(x, pltpu.HBM)
        for x in (kcol, kcount, qslot, owner, dest)
    ]
    return pl.pallas_call(
        terms_kernel,
        out_shape=jax.ShapeDtypeStruct((PIECES, SEND_ROWS, LANES), jnp.bfloat16),
        in_specs=[hbm] * 5 + [vmem] * 7,
        out_specs=vmem,
        scratch_shapes=[
            pltpu.VMEM((EXT, BK, LANES), jnp.bfloat16),
            pltpu.VMEM((TERMS * PIECES, LANES), jnp.float32),
            *(pltpu.SMEM(x.shape, jnp.int32) for x in numbers),
            pltpu.SemaphoreType.DMA((5,)),
        ],
        compiler_params=pltpu.CompilerParams(vmem_limit_bytes=VMEM_LIMIT),
        cost_estimate=pl.CostEstimate(
            flops=1_000_000_000, bytes_accessed=8_000_000, transcendentals=0
        ),
        name="make_terms",
    )(*numbers, squares, turned, prolong, *ghosts)


def sum_kernel(recv_ref, send_ref, value_ref, slot_ref, owner_ref):
    sources, owners = recv_ref.shape[0], send_ref.shape[0]
    width = sources * TERMS
    lane = lax.broadcasted_iota(jnp.int32, (8, LANES), 1)
    tiles = [None] * (width // LANES)
    for s in range(sources):
        value_ref[s * TERMS : (s + 1) * TERMS, :] = recv_ref[s, :TERMS, :]
        labels = recv_ref[s, TERMS:, :].astype(jnp.float32)
        n, start = divmod(s * TERMS, LANES)
        if start:
            labels = pltpu.roll(labels, start, 1)
            tiles[n] = jnp.where(lane >= start, labels, tiles[n])
            if start + TERMS > LANES:
                tiles[n + 1] = labels
        else:
            tiles[n] = labels
    slot = lax.broadcasted_iota(jnp.int32, (NS, LANES), 0).astype(jnp.float32)
    for n, tile in enumerate(tiles):
        at = slice(n * LANES, (n + 1) * LANES)
        owner_ref[:, at] = jnp.broadcast_to(tile[0:1], (16, LANES)).astype(jnp.bfloat16)
        slot_ref[:, at] = (slot == tile[1:2]).astype(jnp.bfloat16)
    values = value_ref[...]
    for o in range(0, owners, SUM_OWNERS):
        chosen = []
        for this in range(o, o + SUM_OWNERS):
            here = jnp.where(owner_ref[...] == this, 1.0, 0.0).astype(jnp.bfloat16)
            chosen += [slot_ref[r : r + 16, :] * here for r in range(0, NS, 16)]
        sums = jnp.dot(
            jnp.concatenate(chosen, 0), values, preferred_element_type=jnp.float32
        ).astype(jnp.bfloat16)
        for n in range(SUM_OWNERS):
            send_ref[o + n] = sums[n * NS : (n + 1) * NS]


def sum_terms(received):
    sources = received.shape[0]
    vmem = pl.BlockSpec(memory_space=pltpu.VMEM)
    return pl.pallas_call(
        sum_kernel,
        out_shape=jax.ShapeDtypeStruct((sources, NS, LANES), jnp.bfloat16),
        in_specs=[vmem],
        out_specs=vmem,
        scratch_shapes=[
            pltpu.VMEM((sources * TERMS, LANES), jnp.bfloat16),
            pltpu.VMEM((NS, sources * TERMS), jnp.bfloat16),
            pltpu.VMEM((16, sources * TERMS), jnp.bfloat16),
        ],
        compiler_params=pltpu.CompilerParams(vmem_limit_bytes=VMEM_LIMIT),
        name="sum_terms",
    )(received)


def join_kernel(recv_ref, out_ref):
    for piece in range(PIECES):
        out_ref[:, piece * LANES : (piece + 1) * LANES] = recv_ref[piece].astype(jnp.float32)


def join_pieces(received):
    vmem = pl.BlockSpec(memory_space=pltpu.VMEM)
    return pl.pallas_call(
        join_kernel,
        out_shape=jax.ShapeDtypeStruct((NS, BP * BP), jnp.float32),
        in_specs=[vmem],
        out_specs=vmem,
        compiler_params=pltpu.CompilerParams(vmem_limit_bytes=VMEM_LIMIT),
        name="join_pieces",
    )(received)


def on_device(stiffness, prolong, kcol, kcount, qslot, glist, owner, dest):
    prolong_rows = prolong[0, 0]
    picked = pick_rows(jnp.transpose(glist[0, 0]), prolong_rows)
    ghosts = []
    for axis, to_lower, to_upper in (("gx", 0, 1), ("yz", 2, 3)):
        size = lax.axis_size(axis)
        up = [(n, n + 1) for n in range(size - 1)]
        down = [(n + 1, n) for n in range(size - 1)]
        ghosts.append(lax.ppermute(picked[to_upper], axis, up))
        ghosts.append(lax.ppermute(picked[to_lower], axis, down))
    squares, turned, own_rows = square_blocks(jnp.transpose(stiffness[0, 0], (1, 0, 2)), prolong_rows)
    packed = make_terms(
        kcol[0, 0],
        kcount[0, 0],
        jnp.transpose(qslot[0, 0], (0, 2, 1)),
        owner[0, 0, :, 0],
        jnp.transpose(dest, (0, 3, 1, 2)),
        squares, turned, own_rows, ghosts,
    )
    received = lax.all_to_all(packed, "yz", split_axis=0, concat_axis=0, tiled=True)
    pieces = lax.all_to_all(sum_terms(received), "yz", split_axis=0, concat_axis=0, tiled=True)
    return join_pieces(pieces)[None, None]


def solution(mesh):
    split = ("gx", "yz")
    in_specs = tuple(P(*split, *(None,) * n) for n in (3, 3, 2, 1, 3, 2, 2, 2))
    return jax.shard_map(
        on_device, mesh=mesh, in_specs=in_specs, out_specs=P(*split, None, None), check_vma=False
    )
```

```python
import functools
import jax
import jax.numpy as jnp
from jax import lax
from jax.experimental import pallas as pl
from jax.experimental.pallas import tpu as pltpu
from jax.sharding import PartitionSpec as P

BK = 96
BP = 64
KW = 27
PW = 2
QW = 3
NB = 8
G = 2
EXT = NB + 4 * G
M = NB * PW
NS = 48
LANES = 128
TERMS = M * QW
PIECES = BP * BP // LANES
SEND_ROWS = TERMS + 8
FLAT_PARTS = ((0, 9), (9, 18), (18, 24), (24, 27))
UNROLL = 3
SUM_OWNERS = 4
VMEM_LIMIT = 20 * 1024 * 1024


def parity(axis):
    return lax.rem(lax.axis_index(axis), 2)


def side_of(swap):
    odd = parity("gx" if swap < 2 else "yz")
    return swap // 2 * 2 + (odd if swap % 2 else 1 - odd)


def swap_pairs(swap, size):
    first = swap % 2
    pairs = [(n, n + 1) for n in range(first, size - 1, 2)]
    return pairs + [(j, i) for i, j in pairs]


def pick_kernel(glist_hbm, prolong_hbm, *refs):
    out_refs, (glist_ref, prolong_ref, sem) = refs[:4], refs[4:]
    copies = [
        pltpu.make_async_copy(glist_hbm, glist_ref, sem.at[0]),
        pltpu.make_async_copy(prolong_hbm, prolong_ref, sem.at[1]),
    ]
    for copy in copies:
        copy.start()
    for copy in copies:
        copy.wait()
    for swap, out_ref in enumerate(out_refs):
        for n in range(G):
            out_ref[n] = prolong_ref[glist_ref[n, side_of(swap)]]


def pick_rows(glist, prolong):
    piece = jax.ShapeDtypeStruct((G, BK, PW * BP), jnp.bfloat16)
    return pl.pallas_call(
        pick_kernel,
        out_shape=[piece] * 4,
        in_specs=[pl.BlockSpec(memory_space=pltpu.HBM)] * 2,
        out_specs=[pl.BlockSpec(memory_space=pltpu.VMEM)] * 4,
        scratch_shapes=[
            pltpu.SMEM((G, 4), jnp.int32),
            pltpu.VMEM((NB, BK, PW * BP), jnp.bfloat16),
            pltpu.SemaphoreType.DMA((2,)),
        ],
        compiler_params=pltpu.CompilerParams(vmem_limit_bytes=VMEM_LIMIT),
        name="pick_rows",
    )(*(pltpu.with_memory_space_constraint(x, pltpu.HBM) for x in (glist, prolong)))


def turn_rows(prolong_ref, turned_ref):
    r_from = lax.broadcasted_iota(jnp.int32, (BK, BK), 0)
    r_to = lax.broadcasted_iota(jnp.int32, (BK, BK), 1)
    row_order = (r_from == (r_to % (BK // 4)) * 4 + r_to // (BK // 4)).astype(jnp.bfloat16)
    c_to = lax.broadcasted_iota(jnp.int32, (LANES, LANES), 0)
    c_from = lax.broadcasted_iota(jnp.int32, (LANES, LANES), 1)
    in_pair = c_to % BP
    column_order = (
        c_from == c_to // BP * BP + (in_pair % (BP // 2)) * 2 + in_pair // (BP // 2)
    ).astype(jnp.bfloat16)
    for i in range(NB):
        turned = lax.dot_general(
            column_order, prolong_ref[i], (((1,), (1,)), ((), ())),
            preferred_element_type=jnp.float32,
        ).astype(jnp.bfloat16)
        turned_ref[i] = jnp.dot(
            turned, row_order, preferred_element_type=jnp.float32
        ).astype(jnp.bfloat16)


def spread_kernel(
    flat_hbm, prolong_hbm, spread_ref, turned_ref, own_ref, prolong_ref, flat_ref, sem, flat_sem
):
    copy = pltpu.make_async_copy(prolong_hbm, prolong_ref, sem)
    parts = [
        pltpu.make_async_copy(flat_hbm.at[a:b], flat_ref.at[a:b], flat_sem.at[n])
        for n, (a, b) in enumerate(FLAT_PARTS)
    ]
    copy.start()
    for part in parts:
        part.start()
    own_ref[:, BK:, :] = jnp.zeros((NB, LANES - BK, LANES), jnp.bfloat16)
    copy.wait()
    own_ref[:, :BK, :] = prolong_ref[...]
    turn_rows(prolong_ref, turned_ref)
    for n, (a, b) in enumerate(FLAT_PARTS):
        parts[n].wait()

        def one_slot(t, carry):
            for c in range(BK * BK // LANES):
                spread_ref[t, c * NB : (c + 1) * NB, :] = flat_ref[
                    t, :, c * LANES : (c + 1) * LANES
                ].astype(jnp.float32)
            return carry

        lax.fori_loop(a, b, one_slot, 0)


def spread_blocks(flat, prolong):
    vmem = pl.BlockSpec(memory_space=pltpu.VMEM)
    return pl.pallas_call(
        spread_kernel,
        out_shape=[
            jax.ShapeDtypeStruct((KW, BK * BK // LANES * NB, LANES), jnp.float32),
            jax.ShapeDtypeStruct((NB, LANES, BK), jnp.bfloat16),
            jax.ShapeDtypeStruct((NB, LANES, LANES), jnp.bfloat16),
        ],
        in_specs=[pl.BlockSpec(memory_space=pltpu.HBM)] * 2,
        out_specs=[vmem] * 3,
        scratch_shapes=[
            pltpu.VMEM(prolong.shape, jnp.bfloat16),
            pltpu.VMEM(flat.shape, jnp.bfloat16),
            pltpu.SemaphoreType.DMA,
            pltpu.SemaphoreType.DMA((len(FLAT_PARTS),)),
        ],
        compiler_params=pltpu.CompilerParams(vmem_limit_bytes=VMEM_LIMIT),
        cost_estimate=pl.CostEstimate(flops=0, bytes_accessed=12_000_000, transcendentals=0),
        name="spread_blocks",
    )(*(pltpu.with_memory_space_constraint(x, pltpu.HBM) for x in (flat, prolong)))


def terms_kernel(
    kcol_hbm, kcount_hbm, qslot_hbm, owner_hbm, dest_hbm,
    spread_ref, turned_ref, own_ref, g0_ref, g1_ref, g2_ref, g3_ref,
    send_ref,
    kcol_ref, kcount_ref, qslot_ref, owner_ref, dest_ref, sem, ext_ref, terms_ref, *sum_refs,
):
    small = [
        pltpu.make_async_copy(source, target, sem.at[n])
        for n, (source, target) in enumerate(
            (
                (kcol_hbm, kcol_ref),
                (kcount_hbm, kcount_ref),
                (qslot_hbm, qslot_ref),
                (owner_hbm, owner_ref),
                (dest_hbm, dest_ref),
            )
        )
    ]
    for copy in small:
        copy.start()
    for sum_ref in sum_refs:
        sum_ref[:QW] = jnp.zeros((QW, BK, LANES), jnp.float32)
    ext_ref[:NB] = own_ref[...]
    ext_ref[NB:, BK:, :] = jnp.zeros((EXT - NB, LANES - BK, LANES), jnp.bfloat16)
    for swap, ghost_ref in enumerate((g0_ref, g1_ref, g2_ref, g3_ref)):
        ext_ref[pl.ds(NB + side_of(swap) * G, G), :BK, :] = ghost_ref[...]
    for copy in small:
        copy.wait()
    lane = lax.broadcasted_iota(jnp.int32, (BK // 4, LANES), 1)

    def one_slot(t):
        for i in range(NB):
            v0, v1, v2 = (
                spread_ref[t, pl.ds(u * NB + i, BK // 4, stride=3 * NB), :] for u in range(3)
            )
            rows = [
                v0,
                pltpu.roll(jnp.where(lane >= 96, v0, v1), 32, 1),
                pltpu.roll(jnp.where(lane >= 64, v1, v2), 64, 1),
                pltpu.roll(v2, 96, 1),
            ]
            product = jnp.dot(
                jnp.concatenate(rows, 0).astype(jnp.bfloat16),
                ext_ref[kcol_ref[i, t]],
                preferred_element_type=jnp.float32,
            )
            live = t < kcount_ref[i]
            for s in range(PW):
                q = jnp.where(live, qslot_ref[i, s, t], QW)
                sum_refs[i * PW + s][q] += product

    def some_slots(step, carry):
        for u in range(UNROLL):
            one_slot(step * UNROLL + u)
        return carry

    lax.fori_loop(0, KW // UNROLL, some_slots, 0)

    left = lax.broadcasted_iota(jnp.int32, (1, LANES), 1) < BP
    for i in range(NB):
        first, second = sum_refs[i * PW], sum_refs[i * PW + 1]
        merged = jnp.concatenate(
            [
                jnp.where(
                    left,
                    first[0] + pltpu.roll(second[0], BP, 1),
                    second[1] + pltpu.roll(first[1], BP, 1),
                ),
                first[2] + pltpu.roll(second[2], BP, 1),
            ],
            1,
        )
        terms = jnp.dot(
            turned_ref[i], merged.astype(jnp.bfloat16), preferred_element_type=jnp.float32
        )
        for a in range(PW):
            even = terms[a * BP : a * BP + BP // 2]
            odd = terms[a * BP + BP // 2 : (a + 1) * BP]
            even_01, even_2 = even[:, :LANES], even[:, LANES:]
            odd_01, odd_2 = odd[:, :LANES], odd[:, LANES:]
            tiles = [
                jnp.where(left, even_01, pltpu.roll(odd_01, BP, 1)),
                jnp.where(left, pltpu.roll(even_01, BP, 1), odd_01),
                jnp.where(left, even_2, pltpu.roll(odd_2, BP, 1)),
            ]
            start = (i * PW + a) * QW * PIECES
            terms_ref[start : start + QW * PIECES, :] = jnp.concatenate(tiles, 0)
    lane = lax.broadcasted_iota(jnp.int32, (1, LANES), 1)
    row = lax.broadcasted_iota(jnp.int32, (8, LANES), 0)
    labels = jnp.zeros((8, LANES), jnp.float32)
    for m in range(M):
        owner = owner_ref[m].astype(jnp.float32)
        for q in range(QW):
            pair = jnp.where(row == 0, owner, dest_ref[0, q, 0, m].astype(jnp.float32))
            labels = jnp.where(lane == m * QW + q, pair, labels)
    labels = labels.astype(jnp.bfloat16)
    for piece in range(PIECES):
        send_ref[piece, :TERMS, :] = jnp.concatenate(
            [
                terms_ref[pl.ds(n * PIECES + piece, 8, stride=PIECES), :]
                for n in range(0, TERMS, 8)
            ],
            0,
        ).astype(jnp.bfloat16)
        send_ref[piece, TERMS:, :] = labels


def make_terms(kcol, kcount, qslot, owner, dest, spread, turned, own, ghosts):
    hbm = pl.BlockSpec(memory_space=pltpu.HBM)
    vmem = pl.BlockSpec(memory_space=pltpu.VMEM)
    numbers = [
        pltpu.with_memory_space_constraint(x, pltpu.HBM)
        for x in (kcol, kcount, qslot, owner, dest)
    ]
    return pl.pallas_call(
        terms_kernel,
        out_shape=jax.ShapeDtypeStruct((PIECES, SEND_ROWS, LANES), jnp.bfloat16),
        in_specs=[hbm] * len(numbers) + [vmem] * 7,
        out_specs=vmem,
        scratch_shapes=[
            *(pltpu.SMEM(x.shape, jnp.int32) for x in numbers),
            pltpu.SemaphoreType.DMA((len(numbers),)),
            pltpu.VMEM((EXT, LANES, LANES), jnp.bfloat16),
            pltpu.VMEM((TERMS * PIECES, LANES), jnp.float32),
            *[pltpu.VMEM((QW + 1, BK, LANES), jnp.float32)] * (NB * PW),
        ],
        compiler_params=pltpu.CompilerParams(vmem_limit_bytes=VMEM_LIMIT),
        cost_estimate=pl.CostEstimate(
            flops=1_000_000_000, bytes_accessed=8_000_000, transcendentals=0
        ),
        name="make_terms",
    )(*numbers, spread, turned, own, *ghosts)


def sum_kernel(recv_ref, send_ref, value_ref, slot_ref, owner_ref):
    sources, owners = recv_ref.shape[0], send_ref.shape[0]
    width = sources * TERMS
    lane = lax.broadcasted_iota(jnp.int32, (8, LANES), 1)
    tiles = [None] * (width // LANES)
    for s in range(sources):
        value_ref[s * TERMS : (s + 1) * TERMS, :] = recv_ref[s, :TERMS, :]
        labels = recv_ref[s, TERMS:, :].astype(jnp.float32)
        n, start = divmod(s * TERMS, LANES)
        if start:
            labels = pltpu.roll(labels, start, 1)
            tiles[n] = jnp.where(lane >= start, labels, tiles[n])
            if start + TERMS > LANES:
                tiles[n + 1] = labels
        else:
            tiles[n] = labels
    slot = lax.broadcasted_iota(jnp.int32, (NS, LANES), 0).astype(jnp.float32)
    for n, tile in enumerate(tiles):
        at = slice(n * LANES, (n + 1) * LANES)
        owner_ref[:, at] = jnp.broadcast_to(tile[0:1], (16, LANES)).astype(jnp.bfloat16)
        slot_ref[:, at] = (slot == tile[1:2]).astype(jnp.bfloat16)
    values = value_ref[...]
    for o in range(0, owners, SUM_OWNERS):
        chosen = []
        for this in range(o, o + SUM_OWNERS):
            here = jnp.where(owner_ref[...] == this, 1.0, 0.0).astype(jnp.bfloat16)
            chosen += [slot_ref[r : r + 16, :] * here for r in range(0, NS, 16)]
        sums = jnp.dot(
            jnp.concatenate(chosen, 0), values, preferred_element_type=jnp.float32
        ).astype(jnp.bfloat16)
        for n in range(SUM_OWNERS):
            send_ref[o + n] = sums[n * NS : (n + 1) * NS]


def sum_terms(received):
    sources = received.shape[0]
    vmem = pl.BlockSpec(memory_space=pltpu.VMEM)
    return pl.pallas_call(
        sum_kernel,
        out_shape=jax.ShapeDtypeStruct((sources, NS, LANES), jnp.bfloat16),
        in_specs=[vmem],
        out_specs=vmem,
        scratch_shapes=[
            pltpu.VMEM((sources * TERMS, LANES), jnp.bfloat16),
            pltpu.VMEM((NS, sources * TERMS), jnp.bfloat16),
            pltpu.VMEM((16, sources * TERMS), jnp.bfloat16),
        ],
        compiler_params=pltpu.CompilerParams(vmem_limit_bytes=VMEM_LIMIT),
        name="sum_terms",
    )(received)


def join_kernel(recv_ref, out_ref):
    for piece in range(PIECES):
        out_ref[:, piece * LANES : (piece + 1) * LANES] = recv_ref[piece].astype(jnp.float32)


def join_pieces(received):
    vmem = pl.BlockSpec(memory_space=pltpu.VMEM)
    return pl.pallas_call(
        join_kernel,
        out_shape=jax.ShapeDtypeStruct((NS, BP * BP), jnp.float32),
        in_specs=[vmem],
        out_specs=vmem,
        compiler_params=pltpu.CompilerParams(vmem_limit_bytes=VMEM_LIMIT),
        name="join_pieces",
    )(received)


def on_device(stiffness, prolong, kcol, kcount, qslot, glist, owner, dest):
    prolong_rows = prolong[0, 0]
    picked = pick_rows(jnp.transpose(glist[0, 0]), prolong_rows)
    ghosts = []
    for swap, rows in enumerate(picked):
        axis = "gx" if swap < 2 else "yz"
        ghosts.append(lax.ppermute(rows, axis, swap_pairs(swap, lax.axis_size(axis))))
    spread, turned, own = spread_blocks(
        jnp.transpose(stiffness[0, 0], (1, 0, 2)), prolong_rows
    )
    packed = make_terms(
        kcol[0, 0],
        kcount[0, 0],
        jnp.transpose(qslot[0, 0], (0, 2, 1)),
        owner[0, 0, :, 0],
        jnp.transpose(dest, (0, 3, 1, 2)),
        spread, turned, own, ghosts,
    )
    received = lax.all_to_all(packed, "yz", split_axis=0, concat_axis=0, tiled=True)
    pieces = lax.all_to_all(sum_terms(received), "yz", split_axis=0, concat_axis=0, tiled=True)
    return join_pieces(pieces)[None, None]


def solution(mesh):
    split = ("gx", "yz")
    in_specs = tuple(P(*split, *(None,) * n) for n in (3, 3, 2, 1, 3, 2, 2, 2))
    return jax.shard_map(
        on_device, mesh=mesh, in_specs=in_specs, out_specs=P(*split, None, None), check_vma=False
    )
```

```python
import functools
import jax
import jax.numpy as jnp
from jax import lax
from jax.experimental import pallas as pl
from jax.experimental.pallas import tpu as pltpu
from jax.sharding import PartitionSpec as P

BK = 96
BP = 64
KW = 27
PW = 2
QW = 3
NB = 8
G = 2
EXT = NB + 4 * G
M = NB * PW
NS = 48
LANES = 128
TERMS = M * QW
PIECES = BP * BP // LANES
SEND_ROWS = TERMS + 8
FLAT_PARTS = ((0, 9), (9, 18), (18, 24), (24, 27))
UNROLL = 3
SUM_OWNERS = 4
VMEM_LIMIT = 20 * 1024 * 1024


def sides():
    odd = lax.rem(lax.axis_index("yz"), 2)
    return 3 - odd, 2 + odd, 1, 0


def send_rows(picked):
    columns, slabs = lax.axis_size("yz"), lax.axis_size("gx")
    even = [(n, n ^ 1) for n in range(columns) if n ^ 1 < columns]
    odd = [(n, (n + 1 ^ 1) - 1) for n in range(1, columns) if n + 1 ^ 1 <= columns]
    up = [(n, (n + 1) % slabs) for n in range(slabs)]
    down = [(j, i) for i, j in up]
    routes = (("yz", even), ("yz", odd), ("gx", up), ("gx", down))
    return [lax.ppermute(rows, *route) for rows, route in zip(picked, routes)]


def pick_kernel(glist_hbm, prolong_hbm, *refs):
    out_refs, (glist_ref, prolong_ref, sem) = refs[:4], refs[4:]
    copies = [
        pltpu.make_async_copy(glist_hbm, glist_ref, sem.at[0]),
        pltpu.make_async_copy(prolong_hbm, prolong_ref, sem.at[1]),
    ]
    for copy in copies:
        copy.start()
    for copy in copies:
        copy.wait()
    for side, out_ref in zip(sides(), out_refs):
        for n in range(G):
            out_ref[n] = prolong_ref[glist_ref[n, side]]


def pick_rows(glist, prolong):
    piece = jax.ShapeDtypeStruct((G, BK, PW * BP), jnp.bfloat16)
    return pl.pallas_call(
        pick_kernel,
        out_shape=[piece] * 4,
        in_specs=[pl.BlockSpec(memory_space=pltpu.HBM)] * 2,
        out_specs=[pl.BlockSpec(memory_space=pltpu.VMEM)] * 4,
        scratch_shapes=[
            pltpu.SMEM((G, 4), jnp.int32),
            pltpu.VMEM((NB, BK, PW * BP), jnp.bfloat16),
            pltpu.SemaphoreType.DMA((2,)),
        ],
        compiler_params=pltpu.CompilerParams(vmem_limit_bytes=VMEM_LIMIT),
        name="pick_rows",
    )(*(pltpu.with_memory_space_constraint(x, pltpu.HBM) for x in (glist, prolong)))


def turn_rows(prolong_ref, turned_ref):
    r_from = lax.broadcasted_iota(jnp.int32, (BK, BK), 0)
    r_to = lax.broadcasted_iota(jnp.int32, (BK, BK), 1)
    row_order = (r_from == (r_to % (BK // 4)) * 4 + r_to // (BK // 4)).astype(jnp.bfloat16)
    c_to = lax.broadcasted_iota(jnp.int32, (LANES, LANES), 0)
    c_from = lax.broadcasted_iota(jnp.int32, (LANES, LANES), 1)
    in_pair = c_to % BP
    column_order = (
        c_from == c_to // BP * BP + (in_pair % (BP // 2)) * 2 + in_pair // (BP // 2)
    ).astype(jnp.bfloat16)
    for i in range(NB):
        turned = lax.dot_general(
            column_order, prolong_ref[i], (((1,), (1,)), ((), ())),
            preferred_element_type=jnp.float32,
        ).astype(jnp.bfloat16)
        turned_ref[i] = jnp.dot(
            turned, row_order, preferred_element_type=jnp.float32
        ).astype(jnp.bfloat16)


def spread_kernel(
    flat_hbm, prolong_hbm, spread_ref, turned_ref, own_ref, prolong_ref, flat_ref, sem, flat_sem
):
    copy = pltpu.make_async_copy(prolong_hbm, prolong_ref, sem)
    parts = [
        pltpu.make_async_copy(flat_hbm.at[a:b], flat_ref.at[a:b], flat_sem.at[n])
        for n, (a, b) in enumerate(FLAT_PARTS)
    ]
    copy.start()
    for part in parts:
        part.start()
    own_ref[:, BK:, :] = jnp.zeros((NB, LANES - BK, LANES), jnp.bfloat16)
    copy.wait()
    own_ref[:, :BK, :] = prolong_ref[...]
    turn_rows(prolong_ref, turned_ref)
    for n, (a, b) in enumerate(FLAT_PARTS):
        parts[n].wait()

        def one_slot(t, carry):
            for c in range(BK * BK // LANES):
                spread_ref[t, c * NB : (c + 1) * NB, :] = flat_ref[
                    t, :, c * LANES : (c + 1) * LANES
                ].astype(jnp.float32)
            return carry

        lax.fori_loop(a, b, one_slot, 0)


def spread_blocks(flat, prolong):
    vmem = pl.BlockSpec(memory_space=pltpu.VMEM)
    return pl.pallas_call(
        spread_kernel,
        out_shape=[
            jax.ShapeDtypeStruct((KW, BK * BK // LANES * NB, LANES), jnp.float32),
            jax.ShapeDtypeStruct((NB, LANES, BK), jnp.bfloat16),
            jax.ShapeDtypeStruct((NB, LANES, LANES), jnp.bfloat16),
        ],
        in_specs=[pl.BlockSpec(memory_space=pltpu.HBM)] * 2,
        out_specs=[vmem] * 3,
        scratch_shapes=[
            pltpu.VMEM(prolong.shape, jnp.bfloat16),
            pltpu.VMEM(flat.shape, jnp.bfloat16),
            pltpu.SemaphoreType.DMA,
            pltpu.SemaphoreType.DMA((len(FLAT_PARTS),)),
        ],
        compiler_params=pltpu.CompilerParams(vmem_limit_bytes=VMEM_LIMIT),
        cost_estimate=pl.CostEstimate(flops=0, bytes_accessed=12_000_000, transcendentals=0),
        name="spread_blocks",
    )(*(pltpu.with_memory_space_constraint(x, pltpu.HBM) for x in (flat, prolong)))


def terms_kernel(
    kcol_hbm, kcount_hbm, qslot_hbm, owner_hbm, dest_hbm,
    spread_ref, turned_ref, own_ref, g0_ref, g1_ref, g2_ref, g3_ref,
    send_ref,
    kcol_ref, kcount_ref, qslot_ref, owner_ref, dest_ref, sem, ext_ref, terms_ref, *sum_refs,
):
    small = [
        pltpu.make_async_copy(source, target, sem.at[n])
        for n, (source, target) in enumerate(
            (
                (kcol_hbm, kcol_ref),
                (kcount_hbm, kcount_ref),
                (qslot_hbm, qslot_ref),
                (owner_hbm, owner_ref),
                (dest_hbm, dest_ref),
            )
        )
    ]
    for copy in small:
        copy.start()
    for sum_ref in sum_refs:
        sum_ref[:QW] = jnp.zeros((QW, BK, LANES), jnp.float32)
    ext_ref[:NB] = own_ref[...]
    ext_ref[NB:, BK:, :] = jnp.zeros((EXT - NB, LANES - BK, LANES), jnp.bfloat16)
    slab = lax.axis_index("gx")
    here = (True, True, slab > 0, slab < lax.axis_size("gx") - 1)
    from_side = (*sides()[:2], 0, 1)
    for ghost_ref, side, exists in zip((g0_ref, g1_ref, g2_ref, g3_ref), from_side, here):
        rows = ghost_ref[...]
        ext_ref[pl.ds(NB + side * G, G), :BK, :] = jnp.where(exists, rows, jnp.zeros_like(rows))
    for copy in small:
        copy.wait()
    lane = lax.broadcasted_iota(jnp.int32, (BK // 4, LANES), 1)

    def one_slot(t):
        for i in range(NB):
            v0, v1, v2 = (
                spread_ref[t, pl.ds(u * NB + i, BK // 4, stride=3 * NB), :] for u in range(3)
            )
            rows = [
                v0,
                pltpu.roll(jnp.where(lane >= 96, v0, v1), 32, 1),
                pltpu.roll(jnp.where(lane >= 64, v1, v2), 64, 1),
                pltpu.roll(v2, 96, 1),
            ]
            product = jnp.dot(
                jnp.concatenate(rows, 0).astype(jnp.bfloat16),
                ext_ref[kcol_ref[i, t]],
                preferred_element_type=jnp.float32,
            )
            live = t < kcount_ref[i]
            for s in range(PW):
                q = jnp.where(live, qslot_ref[i, s, t], QW)
                sum_refs[i * PW + s][q] += product

    def some_slots(step, carry):
        for u in range(UNROLL):
            one_slot(step * UNROLL + u)
        return carry

    lax.fori_loop(0, KW // UNROLL, some_slots, 0)

    left = lax.broadcasted_iota(jnp.int32, (1, LANES), 1) < BP
    for i in range(NB):
        first, second = sum_refs[i * PW], sum_refs[i * PW + 1]
        merged = jnp.concatenate(
            [
                jnp.where(
                    left,
                    first[0] + pltpu.roll(second[0], BP, 1),
                    second[1] + pltpu.roll(first[1], BP, 1),
                ),
                first[2] + pltpu.roll(second[2], BP, 1),
            ],
            1,
        )
        terms = jnp.dot(
            turned_ref[i], merged.astype(jnp.bfloat16), preferred_element_type=jnp.float32
        )
        for a in range(PW):
            even = terms[a * BP : a * BP + BP // 2]
            odd = terms[a * BP + BP // 2 : (a + 1) * BP]
            even_01, even_2 = even[:, :LANES], even[:, LANES:]
            odd_01, odd_2 = odd[:, :LANES], odd[:, LANES:]
            tiles = [
                jnp.where(left, even_01, pltpu.roll(odd_01, BP, 1)),
                jnp.where(left, pltpu.roll(even_01, BP, 1), odd_01),
                jnp.where(left, even_2, pltpu.roll(odd_2, BP, 1)),
            ]
            start = (i * PW + a) * QW * PIECES
            terms_ref[start : start + QW * PIECES, :] = jnp.concatenate(tiles, 0)
    lane = lax.broadcasted_iota(jnp.int32, (1, LANES), 1)
    row = lax.broadcasted_iota(jnp.int32, (8, LANES), 0)
    labels = jnp.zeros((8, LANES), jnp.float32)
    for m in range(M):
        owner = owner_ref[m].astype(jnp.float32)
        for q in range(QW):
            pair = jnp.where(row == 0, owner, dest_ref[0, q, 0, m].astype(jnp.float32))
            labels = jnp.where(lane == m * QW + q, pair, labels)
    labels = labels.astype(jnp.bfloat16)
    for piece in range(PIECES):
        send_ref[piece, :TERMS, :] = jnp.concatenate(
            [
                terms_ref[pl.ds(n * PIECES + piece, 8, stride=PIECES), :]
                for n in range(0, TERMS, 8)
            ],
            0,
        ).astype(jnp.bfloat16)
        send_ref[piece, TERMS:, :] = labels


def make_terms(kcol, kcount, qslot, owner, dest, spread, turned, own, ghosts):
    hbm = pl.BlockSpec(memory_space=pltpu.HBM)
    vmem = pl.BlockSpec(memory_space=pltpu.VMEM)
    numbers = [
        pltpu.with_memory_space_constraint(x, pltpu.HBM)
        for x in (kcol, kcount, qslot, owner, dest)
    ]
    return pl.pallas_call(
        terms_kernel,
        out_shape=jax.ShapeDtypeStruct((PIECES, SEND_ROWS, LANES), jnp.bfloat16),
        in_specs=[hbm] * len(numbers) + [vmem] * 7,
        out_specs=vmem,
        scratch_shapes=[
            *(pltpu.SMEM(x.shape, jnp.int32) for x in numbers),
            pltpu.SemaphoreType.DMA((len(numbers),)),
            pltpu.VMEM((EXT, LANES, LANES), jnp.bfloat16),
            pltpu.VMEM((TERMS * PIECES, LANES), jnp.float32),
            *[pltpu.VMEM((QW + 1, BK, LANES), jnp.float32)] * (NB * PW),
        ],
        compiler_params=pltpu.CompilerParams(vmem_limit_bytes=VMEM_LIMIT),
        cost_estimate=pl.CostEstimate(
            flops=1_000_000_000, bytes_accessed=8_000_000, transcendentals=0
        ),
        name="make_terms",
    )(*numbers, spread, turned, own, *ghosts)


def sum_kernel(recv_ref, send_ref, value_ref, slot_ref, owner_ref):
    sources, owners = recv_ref.shape[0], send_ref.shape[0]
    width = sources * TERMS
    lane = lax.broadcasted_iota(jnp.int32, (8, LANES), 1)
    tiles = [None] * (width // LANES)
    for s in range(sources):
        value_ref[s * TERMS : (s + 1) * TERMS, :] = recv_ref[s, :TERMS, :]
        labels = recv_ref[s, TERMS:, :].astype(jnp.float32)
        n, start = divmod(s * TERMS, LANES)
        if start:
            labels = pltpu.roll(labels, start, 1)
            tiles[n] = jnp.where(lane >= start, labels, tiles[n])
            if start + TERMS > LANES:
                tiles[n + 1] = labels
        else:
            tiles[n] = labels
    slot = lax.broadcasted_iota(jnp.int32, (NS, LANES), 0).astype(jnp.float32)
    for n, tile in enumerate(tiles):
        at = slice(n * LANES, (n + 1) * LANES)
        owner_ref[:, at] = jnp.broadcast_to(tile[0:1], (16, LANES)).astype(jnp.bfloat16)
        slot_ref[:, at] = (slot == tile[1:2]).astype(jnp.bfloat16)
    values = value_ref[...]
    for o in range(0, owners, SUM_OWNERS):
        chosen = []
        for this in range(o, o + SUM_OWNERS):
            here = jnp.where(owner_ref[...] == this, 1.0, 0.0).astype(jnp.bfloat16)
            chosen += [slot_ref[r : r + 16, :] * here for r in range(0, NS, 16)]
        sums = jnp.dot(
            jnp.concatenate(chosen, 0), values, preferred_element_type=jnp.float32
        ).astype(jnp.bfloat16)
        for n in range(SUM_OWNERS):
            send_ref[o + n] = sums[n * NS : (n + 1) * NS]


def sum_terms(received):
    sources = received.shape[0]
    vmem = pl.BlockSpec(memory_space=pltpu.VMEM)
    return pl.pallas_call(
        sum_kernel,
        out_shape=jax.ShapeDtypeStruct((sources, NS, LANES), jnp.bfloat16),
        in_specs=[vmem],
        out_specs=vmem,
        scratch_shapes=[
            pltpu.VMEM((sources * TERMS, LANES), jnp.bfloat16),
            pltpu.VMEM((NS, sources * TERMS), jnp.bfloat16),
            pltpu.VMEM((16, sources * TERMS), jnp.bfloat16),
        ],
        compiler_params=pltpu.CompilerParams(vmem_limit_bytes=VMEM_LIMIT),
        name="sum_terms",
    )(received)


def join_kernel(recv_ref, out_ref):
    for piece in range(PIECES):
        out_ref[:, piece * LANES : (piece + 1) * LANES] = recv_ref[piece].astype(jnp.float32)


def join_pieces(received):
    vmem = pl.BlockSpec(memory_space=pltpu.VMEM)
    return pl.pallas_call(
        join_kernel,
        out_shape=jax.ShapeDtypeStruct((NS, BP * BP), jnp.float32),
        in_specs=[vmem],
        out_specs=vmem,
        compiler_params=pltpu.CompilerParams(vmem_limit_bytes=VMEM_LIMIT),
        name="join_pieces",
    )(received)


def on_device(stiffness, prolong, kcol, kcount, qslot, glist, owner, dest):
    prolong_rows = prolong[0, 0]
    picked = pick_rows(jnp.transpose(glist[0, 0]), prolong_rows)
    ghosts = send_rows(picked)
    spread, turned, own = spread_blocks(
        jnp.transpose(stiffness[0, 0], (1, 0, 2)), prolong_rows
    )
    packed = make_terms(
        kcol[0, 0],
        kcount[0, 0],
        jnp.transpose(qslot[0, 0], (0, 2, 1)),
        owner[0, 0, :, 0],
        jnp.transpose(dest, (0, 3, 1, 2)),
        spread, turned, own, ghosts,
    )
    received = lax.all_to_all(packed, "yz", split_axis=0, concat_axis=0, tiled=True)
    pieces = lax.all_to_all(sum_terms(received), "yz", split_axis=0, concat_axis=0, tiled=True)
    return join_pieces(pieces)[None, None]


def solution(mesh):
    split = ("gx", "yz")
    in_specs = tuple(P(*split, *(None,) * n) for n in (3, 3, 2, 1, 3, 2, 2, 2))
    return jax.shard_map(
        on_device, mesh=mesh, in_specs=in_specs, out_specs=P(*split, None, None), check_vma=False
    )
```

```python
import functools
import jax
import jax.numpy as jnp
from jax import lax
from jax.experimental import pallas as pl
from jax.experimental.pallas import tpu as pltpu
from jax.sharding import PartitionSpec as P

BK = 96
BP = 64
KW = 27
PW = 2
QW = 3
NB = 8
G = 2
EXT = NB + 4 * G
M = NB * PW
NS = 48
LANES = 128
TERMS = M * QW
PIECES = BP * BP // LANES
SEND_ROWS = TERMS + 8
FLAT_PARTS = tuple((t, t + 3) for t in range(0, KW, 3))
UNROLL = 3
SUM_OWNERS = 4
VMEM_LIMIT = 20 * 1024 * 1024


def sides():
    odd = lax.rem(lax.axis_index("yz"), 2)
    return 3 - odd, 2 + odd, 1, 0


def send_rows(picked):
    columns, slabs = lax.axis_size("yz"), lax.axis_size("gx")
    even = [(n, n ^ 1) for n in range(columns) if n ^ 1 < columns]
    odd = [(n, (n + 1 ^ 1) - 1) for n in range(1, columns) if n + 1 ^ 1 <= columns]
    up = [(n, (n + 1) % slabs) for n in range(slabs)]
    down = [(j, i) for i, j in up]
    routes = (("yz", even), ("yz", odd), ("gx", up), ("gx", down))
    return [lax.ppermute(rows, *route) for rows, route in zip(picked, routes)]


def pick_kernel(glist_hbm, prolong_hbm, *refs):
    out_refs, (glist_ref, prolong_ref, sem) = refs[:4], refs[4:]
    copies = [
        pltpu.make_async_copy(glist_hbm, glist_ref, sem.at[0]),
        pltpu.make_async_copy(prolong_hbm, prolong_ref, sem.at[1]),
    ]
    for copy in copies:
        copy.start()
    for copy in copies:
        copy.wait()
    for side, out_ref in zip(sides(), out_refs):
        for n in range(G):
            out_ref[n] = prolong_ref[glist_ref[n, side]]


def pick_rows(glist, prolong):
    piece = jax.ShapeDtypeStruct((G, BK, PW * BP), jnp.bfloat16)
    return pl.pallas_call(
        pick_kernel,
        out_shape=[piece] * 4,
        in_specs=[pl.BlockSpec(memory_space=pltpu.HBM)] * 2,
        out_specs=[pl.BlockSpec(memory_space=pltpu.VMEM)] * 4,
        scratch_shapes=[
            pltpu.SMEM((G, 4), jnp.int32),
            pltpu.VMEM((NB, BK, PW * BP), jnp.bfloat16),
            pltpu.SemaphoreType.DMA((2,)),
        ],
        compiler_params=pltpu.CompilerParams(vmem_limit_bytes=VMEM_LIMIT),
        name="pick_rows",
    )(*(pltpu.with_memory_space_constraint(x, pltpu.HBM) for x in (glist, prolong)))


def turn_rows(prolong_ref, turned_ref):
    r_from = lax.broadcasted_iota(jnp.int32, (BK, BK), 0)
    r_to = lax.broadcasted_iota(jnp.int32, (BK, BK), 1)
    row_order = (r_from == (r_to % (BK // 4)) * 4 + r_to // (BK // 4)).astype(jnp.bfloat16)
    c_to = lax.broadcasted_iota(jnp.int32, (LANES, LANES), 0)
    c_from = lax.broadcasted_iota(jnp.int32, (LANES, LANES), 1)
    in_pair = c_to % BP
    column_order = (
        c_from == c_to // BP * BP + (in_pair % (BP // 2)) * 2 + in_pair // (BP // 2)
    ).astype(jnp.bfloat16)
    for i in range(NB):
        turned = lax.dot_general(
            column_order, prolong_ref[i], (((1,), (1,)), ((), ())),
            preferred_element_type=jnp.float32,
        ).astype(jnp.bfloat16)
        turned_ref[i] = jnp.dot(
            turned, row_order, preferred_element_type=jnp.float32
        ).astype(jnp.bfloat16)


def spread_kernel(
    flat_hbm, prolong_hbm, spread_ref, turned_ref, own_ref, prolong_ref, flat_ref, sem, flat_sem
):
    copy = pltpu.make_async_copy(prolong_hbm, prolong_ref, sem)
    parts = [
        pltpu.make_async_copy(flat_hbm.at[a:b], flat_ref.at[a:b], flat_sem.at[n])
        for n, (a, b) in enumerate(FLAT_PARTS)
    ]
    copy.start()
    for part in parts:
        part.start()
    own_ref[:, BK:, :] = jnp.zeros((NB, LANES - BK, LANES), jnp.bfloat16)
    copy.wait()
    own_ref[:, :BK, :] = prolong_ref[...]
    turn_rows(prolong_ref, turned_ref)
    for n, (a, b) in enumerate(FLAT_PARTS):
        parts[n].wait()

        for t in range(a, b):
            for c in range(BK * BK // LANES):
                spread_ref[t, c * NB : (c + 1) * NB, :] = flat_ref[
                    t, :, c * LANES : (c + 1) * LANES
                ].astype(jnp.float32)


def spread_blocks(flat, prolong):
    vmem = pl.BlockSpec(memory_space=pltpu.VMEM)
    return pl.pallas_call(
        spread_kernel,
        out_shape=[
            jax.ShapeDtypeStruct((KW, BK * BK // LANES * NB, LANES), jnp.float32),
            jax.ShapeDtypeStruct((NB, LANES, BK), jnp.bfloat16),
            jax.ShapeDtypeStruct((NB, LANES, LANES), jnp.bfloat16),
        ],
        in_specs=[pl.BlockSpec(memory_space=pltpu.HBM)] * 2,
        out_specs=[vmem] * 3,
        scratch_shapes=[
            pltpu.VMEM(prolong.shape, jnp.bfloat16),
            pltpu.VMEM(flat.shape, jnp.bfloat16),
            pltpu.SemaphoreType.DMA,
            pltpu.SemaphoreType.DMA((len(FLAT_PARTS),)),
        ],
        compiler_params=pltpu.CompilerParams(vmem_limit_bytes=VMEM_LIMIT),
        cost_estimate=pl.CostEstimate(flops=0, bytes_accessed=12_000_000, transcendentals=0),
        name="spread_blocks",
    )(*(pltpu.with_memory_space_constraint(x, pltpu.HBM) for x in (flat, prolong)))


def terms_kernel(
    kcol_hbm, kcount_hbm, qslot_hbm, owner_hbm, dest_hbm,
    spread_ref, turned_ref, own_ref, g0_ref, g1_ref, g2_ref, g3_ref,
    send_ref,
    kcol_ref, kcount_ref, qslot_ref, owner_ref, dest_ref, sem, ext_ref, terms_ref, *sum_refs,
):
    small = [
        pltpu.make_async_copy(source, target, sem.at[n])
        for n, (source, target) in enumerate(
            (
                (kcol_hbm, kcol_ref),
                (kcount_hbm, kcount_ref),
                (qslot_hbm, qslot_ref),
                (owner_hbm, owner_ref),
                (dest_hbm, dest_ref),
            )
        )
    ]
    for copy in small:
        copy.start()
    for sum_ref in sum_refs:
        sum_ref[:QW] = jnp.zeros((QW, BK, LANES), jnp.float32)
    ext_ref[:NB] = own_ref[...]
    ext_ref[NB:, BK:, :] = jnp.zeros((EXT - NB, LANES - BK, LANES), jnp.bfloat16)
    slab = lax.axis_index("gx")
    here = (True, True, slab > 0, slab < lax.axis_size("gx") - 1)
    from_side = (*sides()[:2], 0, 1)
    for ghost_ref, side, exists in zip((g0_ref, g1_ref, g2_ref, g3_ref), from_side, here):
        rows = ghost_ref[...]
        ext_ref[pl.ds(NB + side * G, G), :BK, :] = jnp.where(exists, rows, jnp.zeros_like(rows))
    for copy in small:
        copy.wait()
    lane = lax.broadcasted_iota(jnp.int32, (BK // 4, LANES), 1)

    def one_slot(t):
        for i in range(NB):
            v0, v1, v2 = (
                spread_ref[t, pl.ds(u * NB + i, BK // 4, stride=3 * NB), :] for u in range(3)
            )
            rows = [
                v0,
                pltpu.roll(jnp.where(lane >= 96, v0, v1), 32, 1),
                pltpu.roll(jnp.where(lane >= 64, v1, v2), 64, 1),
                pltpu.roll(v2, 96, 1),
            ]
            product = jnp.dot(
                jnp.concatenate(rows, 0).astype(jnp.bfloat16),
                ext_ref[kcol_ref[i, t]],
                preferred_element_type=jnp.float32,
            )
            live = t < kcount_ref[i]
            for s in range(PW):
                q = jnp.where(live, qslot_ref[i, s, t], QW)
                sum_refs[i * PW + s][q] += product

    def some_slots(step, carry):
        for u in range(UNROLL):
            one_slot(step * UNROLL + u)
        return carry

    lax.fori_loop(0, KW // UNROLL, some_slots, 0)

    left = lax.broadcasted_iota(jnp.int32, (1, LANES), 1) < BP
    for i in range(NB):
        first, second = sum_refs[i * PW], sum_refs[i * PW + 1]
        merged = jnp.concatenate(
            [
                jnp.where(
                    left,
                    first[0] + pltpu.roll(second[0], BP, 1),
                    second[1] + pltpu.roll(first[1], BP, 1),
                ),
                first[2] + pltpu.roll(second[2], BP, 1),
            ],
            1,
        )
        terms = jnp.dot(
            turned_ref[i], merged.astype(jnp.bfloat16), preferred_element_type=jnp.float32
        )
        for a in range(PW):
            even = terms[a * BP : a * BP + BP // 2]
            odd = terms[a * BP + BP // 2 : (a + 1) * BP]
            even_01, even_2 = even[:, :LANES], even[:, LANES:]
            odd_01, odd_2 = odd[:, :LANES], odd[:, LANES:]
            tiles = [
                jnp.where(left, even_01, pltpu.roll(odd_01, BP, 1)),
                jnp.where(left, pltpu.roll(even_01, BP, 1), odd_01),
                jnp.where(left, even_2, pltpu.roll(odd_2, BP, 1)),
            ]
            start = (i * PW + a) * QW * PIECES
            terms_ref[start : start + QW * PIECES, :] = jnp.concatenate(tiles, 0)
    lane = lax.broadcasted_iota(jnp.int32, (1, LANES), 1)
    row = lax.broadcasted_iota(jnp.int32, (8, LANES), 0)
    labels = jnp.zeros((8, LANES), jnp.float32)
    for m in range(M):
        owner = owner_ref[m].astype(jnp.float32)
        for q in range(QW):
            pair = jnp.where(row == 0, owner, dest_ref[0, q, 0, m].astype(jnp.float32))
            labels = jnp.where(lane == m * QW + q, pair, labels)
    labels = labels.astype(jnp.bfloat16)
    for piece in range(PIECES):
        send_ref[piece, :TERMS, :] = jnp.concatenate(
            [
                terms_ref[pl.ds(n * PIECES + piece, 8, stride=PIECES), :]
                for n in range(0, TERMS, 8)
            ],
            0,
        ).astype(jnp.bfloat16)
        send_ref[piece, TERMS:, :] = labels


def make_terms(kcol, kcount, qslot, owner, dest, spread, turned, own, ghosts):
    hbm = pl.BlockSpec(memory_space=pltpu.HBM)
    vmem = pl.BlockSpec(memory_space=pltpu.VMEM)
    numbers = [
        pltpu.with_memory_space_constraint(x, pltpu.HBM)
        for x in (kcol, kcount, qslot, owner, dest)
    ]
    return pl.pallas_call(
        terms_kernel,
        out_shape=jax.ShapeDtypeStruct((PIECES, SEND_ROWS, LANES), jnp.bfloat16),
        in_specs=[hbm] * len(numbers) + [vmem] * 7,
        out_specs=vmem,
        scratch_shapes=[
            *(pltpu.SMEM(x.shape, jnp.int32) for x in numbers),
            pltpu.SemaphoreType.DMA((len(numbers),)),
            pltpu.VMEM((EXT, LANES, LANES), jnp.bfloat16),
            pltpu.VMEM((TERMS * PIECES, LANES), jnp.float32),
            *[pltpu.VMEM((QW + 1, BK, LANES), jnp.float32)] * (NB * PW),
        ],
        compiler_params=pltpu.CompilerParams(vmem_limit_bytes=VMEM_LIMIT),
        cost_estimate=pl.CostEstimate(
            flops=1_000_000_000, bytes_accessed=8_000_000, transcendentals=0
        ),
        name="make_terms",
    )(*numbers, spread, turned, own, *ghosts)


def sum_kernel(recv_ref, send_ref, value_ref, slot_ref, owner_ref):
    sources, owners = recv_ref.shape[0], send_ref.shape[0]
    width = sources * TERMS
    lane = lax.broadcasted_iota(jnp.int32, (8, LANES), 1)
    tiles = [None] * (width // LANES)
    for s in range(sources):
        value_ref[s * TERMS : (s + 1) * TERMS, :] = recv_ref[s, :TERMS, :]
        labels = recv_ref[s, TERMS:, :].astype(jnp.float32)
        n, start = divmod(s * TERMS, LANES)
        if start:
            labels = pltpu.roll(labels, start, 1)
            tiles[n] = jnp.where(lane >= start, labels, tiles[n])
            if start + TERMS > LANES:
                tiles[n + 1] = labels
        else:
            tiles[n] = labels
    slot = lax.broadcasted_iota(jnp.int32, (NS, LANES), 0).astype(jnp.float32)
    for n, tile in enumerate(tiles):
        at = slice(n * LANES, (n + 1) * LANES)
        owner_ref[:, at] = jnp.broadcast_to(tile[0:1], (16, LANES)).astype(jnp.bfloat16)
        slot_ref[:, at] = (slot == tile[1:2]).astype(jnp.bfloat16)
    values = value_ref[...]
    for o in range(0, owners, SUM_OWNERS):
        chosen = []
        for this in range(o, o + SUM_OWNERS):
            here = jnp.where(owner_ref[...] == this, 1.0, 0.0).astype(jnp.bfloat16)
            chosen += [slot_ref[r : r + 16, :] * here for r in range(0, NS, 16)]
        sums = jnp.dot(
            jnp.concatenate(chosen, 0), values, preferred_element_type=jnp.float32
        ).astype(jnp.bfloat16)
        for n in range(SUM_OWNERS):
            send_ref[o + n] = sums[n * NS : (n + 1) * NS]


def sum_terms(received):
    sources = received.shape[0]
    vmem = pl.BlockSpec(memory_space=pltpu.VMEM)
    return pl.pallas_call(
        sum_kernel,
        out_shape=jax.ShapeDtypeStruct((sources, NS, LANES), jnp.bfloat16),
        in_specs=[vmem],
        out_specs=vmem,
        scratch_shapes=[
            pltpu.VMEM((sources * TERMS, LANES), jnp.bfloat16),
            pltpu.VMEM((NS, sources * TERMS), jnp.bfloat16),
            pltpu.VMEM((16, sources * TERMS), jnp.bfloat16),
        ],
        compiler_params=pltpu.CompilerParams(vmem_limit_bytes=VMEM_LIMIT),
        name="sum_terms",
    )(received)


def join_kernel(recv_ref, out_ref):
    for piece in range(PIECES):
        out_ref[:, piece * LANES : (piece + 1) * LANES] = recv_ref[piece].astype(jnp.float32)


def join_pieces(received):
    vmem = pl.BlockSpec(memory_space=pltpu.VMEM)
    return pl.pallas_call(
        join_kernel,
        out_shape=jax.ShapeDtypeStruct((NS, BP * BP), jnp.float32),
        in_specs=[vmem],
        out_specs=vmem,
        compiler_params=pltpu.CompilerParams(vmem_limit_bytes=VMEM_LIMIT),
        name="join_pieces",
    )(received)


def on_device(stiffness, prolong, kcol, kcount, qslot, glist, owner, dest):
    prolong_rows = prolong[0, 0]
    picked = pick_rows(jnp.transpose(glist[0, 0]), prolong_rows)
    ghosts = send_rows(picked)
    spread, turned, own = spread_blocks(
        jnp.transpose(stiffness[0, 0], (1, 0, 2)), prolong_rows
    )
    packed = make_terms(
        kcol[0, 0],
        kcount[0, 0],
        jnp.transpose(qslot[0, 0], (0, 2, 1)),
        owner[0, 0, :, 0],
        jnp.transpose(dest, (0, 3, 1, 2)),
        spread, turned, own, ghosts,
    )
    received = lax.all_to_all(packed, "yz", split_axis=0, concat_axis=0, tiled=True)
    pieces = lax.all_to_all(sum_terms(received), "yz", split_axis=0, concat_axis=0, tiled=True)
    return join_pieces(pieces)[None, None]


def solution(mesh):
    split = ("gx", "yz")
    in_specs = tuple(P(*split, *(None,) * n) for n in (3, 3, 2, 1, 3, 2, 2, 2))
    return jax.shard_map(
        on_device, mesh=mesh, in_specs=in_specs, out_specs=P(*split, None, None), check_vma=False
    )
```
